32 devices in a mesh: row: 2 (over core), col: 16 (over z, y, x).
Axes of the slice: x: 2, y: 2, z: 4, core: 2. Of those that a mesh axis runs over, the one named last changes fastest.
Arguments:
- image: bfloat16 [32, 512, 768], P('row', 'col'), may hold values from -6 to 6
- dw_kernel: float32 [768, 49], replicated, may hold values from -0.875 to 0.875
- ln_gain: float32 [768], replicated, may hold values from 0.25 to 1.75
- w_in: bfloat16 [768, 3072], P('col'), may hold values from -0.21875 to 0.21875
- b_in: float32 [3072], replicated, may hold values from -3 to 3
- w_out: bfloat16 [3072, 768], P('col'), may hold values from -0.109375 to 0.109375
- layer_scale: float32 [768], replicated, may hold values from 0.5 to 1.5
- cotangent: bfloat16 [32, 512, 768], P('row', 'col'), may hold values from -8 to 8
Outputs:
- out_map: bfloat16 [32, 512, 768], P('row', 'col')
- grad_image: bfloat16 [32, 512, 768], P('row', 'col')
- grad_kernel: float32 [768, 49], P(('row', 'col'))
- grad_w_in: float32 [768, 3072], P('col')
- grad_w_out: float32 [3072, 768], P('col')
- grad_b_in: float32 [3072], replicated
- grad_gain: float32 [768], replicated
- grad_scale: float32 [768], replicated
The draws below stay inside these ranges and needn't reach their ends.
All inputs are finite; a program needn't handle non-finite values.
Results may differ from the reference program's by a relative error of at most 0.0071.
Values may be sent and summed in bfloat16 or wider, within the bound.
A program may use at most 128 MiB of HBM per device.

```python
import math
import jax
import jax.numpy as jnp
from jax import lax

D = 768
FF = 3072
KSIZE = 7
DILATE = 2
REACH = 6
MAP_ROWS = 32
MAP_COLS = 512


def draw_cotangent(key, part):
    row_place = jnp.arange(MAP_ROWS, dtype=jnp.float32)[:, None, None] / MAP_ROWS
    col_place = jnp.arange(MAP_COLS, dtype=jnp.float32)[None, :, None] / MAP_COLS
    ramp = 0.5 + row_place + 0.5 * col_place
    base = jax.random.truncated_normal(key, -4.0, 4.0, (MAP_ROWS, MAP_COLS, D), jnp.float32)
    return (base * ramp).astype(jnp.bfloat16)


def steps_of(own_key, shape, cuts, smallest, top_value):
    factor_of, own = 1.0, jax.random.fold_in(own_key, 6)
    for dim, blocks in cuts:
        draws = jnp.exp(jax.random.uniform(jax.random.fold_in(own, dim), (blocks,), jnp.float32, smallest / len(cuts), top_value / len(cuts)))
        factor_of = factor_of * jnp.repeat(draws, shape[dim] // blocks).reshape([-1 if axis == dim else 1 for axis in range(len(shape))])
    return factor_of


def noise(rng, shape, spread, bound, split=(), kind=jnp.bfloat16):
    level = steps_of(rng, shape, split, -0.22, 0.18) if split else 1.0
    result = jax.random.normal(rng, shape, jnp.float32) * spread * level
    return jnp.minimum(jnp.maximum(result, -bound), bound).astype(kind)


def setup_inputs(seed: int = 0) -> dict:
    keys = jax.random.split(jax.random.key(seed), 9)
    image = noise(keys[0], (MAP_ROWS, MAP_COLS, D), 1.0, 6.0, ((0, 2), (1, 16)))
    dw_kernel = noise(keys[1], (D, KSIZE * KSIZE), (KSIZE * KSIZE) ** -0.5, 0.875, (), jnp.float32)
    ln_gain = jnp.clip(1.0 + 0.15 * jax.random.normal(keys[2], (D,), jnp.float32), 0.25, 1.75)
    w_in = noise(keys[3], (D, FF), D ** -0.5, 0.21875, ((0, 16),))
    b_in = noise(keys[4], (FF,), 0.5, 3.0, (), jnp.float32)
    w_out = noise(keys[5], (FF, D), FF ** -0.5, 0.109375, ((0, 16),))
    layer_scale = jnp.clip(jax.random.uniform(keys[6], (D,), jnp.float32, 0.5, 1.5), 0.5, 1.5)
    cotangent = draw_cotangent(jax.random.fold_in(keys[8], 71), 0)
    return dict(image=image, dw_kernel=dw_kernel, ln_gain=ln_gain, w_in=w_in, b_in=b_in, w_out=w_out, layer_scale=layer_scale, cotangent=cotangent)


EPSILON = 1e-06

def normal_cdf(values):
    return 0.5 * (1.0 + jax.scipy.special.erf(values * 0.7071067811865476))

def gelu_exact(values):
    return values * normal_cdf(values)

def gelu_slope(values):
    return normal_cdf(values) + values * jnp.exp(-0.5 * values * values) * 0.3989422804014327

def spatial_stencil(padded, tap_table, height, breadth):
    summed = jnp.zeros((height, breadth, tap_table.shape[0]), jnp.float32)
    for tap_row in range(KSIZE):
        for tap_col in range(KSIZE):
            window = padded[DILATE * tap_row:DILATE * tap_row + height, DILATE * tap_col:DILATE * tap_col + breadth, :].astype(jnp.float32)
            summed = summed + tap_table[:, KSIZE * tap_row + tap_col] * window
    return summed

def spatial_taps(padded, gradient, height, breadth):
    columns = []
    for tap_row in range(KSIZE):
        for tap_col in range(KSIZE):
            window = padded[DILATE * tap_row:DILATE * tap_row + height, DILATE * tap_col:DILATE * tap_col + breadth, :].astype(jnp.float32)
            columns.append(lax.optimization_barrier(jnp.sum(gradient * window, axis=(0, 1))))
    return jnp.stack(columns, axis=1)

def reference(image, dw_kernel, ln_gain, w_in, b_in, w_out, layer_scale, cotangent):
    height, breadth, channels = image.shape
    hidden_units = w_in.shape[1]
    pixels = height * breadth
    scale_factor = 1.0 / math.sqrt(pixels)
    padded = jnp.pad(image, ((REACH, REACH), (REACH, REACH), (0, 0)))
    conv_map = spatial_stencil(padded, dw_kernel, height, breadth).astype(jnp.bfloat16)
    conv_rows = conv_map.astype(jnp.float32).reshape(pixels, channels)
    average = lax.optimization_barrier(jnp.mean(conv_rows, axis=1, keepdims=True))
    centered = conv_rows - average
    inverse = lax.rsqrt(lax.optimization_barrier(jnp.mean(centered * centered, axis=1, keepdims=True)) + EPSILON)
    standard = centered * inverse
    normed = (standard * ln_gain).astype(jnp.bfloat16)
    block = math.gcd(pixels, 4096)

    def block_step(carry, pieces):
        sum_in, sum_out, sum_bias, sum_scale = carry
        normed_block, upstream_block, image_block = pieces
        preact = jnp.dot(normed_block, w_in, preferred_element_type=jnp.float32) + b_in
        hidden = gelu_exact(preact).astype(jnp.bfloat16)
        mixed = jnp.dot(hidden, w_out, preferred_element_type=jnp.float32)
        out_block = (image_block.astype(jnp.float32) + layer_scale * mixed).astype(jnp.bfloat16)
        upstream = upstream_block.astype(jnp.float32)
        sum_scale = sum_scale + lax.optimization_barrier(jnp.sum(upstream * mixed, axis=0))
        grad_mix = (upstream * layer_scale).astype(jnp.bfloat16)
        sum_out = sum_out + jnp.dot(hidden.T, grad_mix, preferred_element_type=jnp.float32)
        grad_hidden = jnp.dot(grad_mix, w_out.T, preferred_element_type=jnp.float32)
        grad_pre = grad_hidden * gelu_slope(preact)
        sum_bias = sum_bias + lax.optimization_barrier(jnp.sum(grad_pre, axis=0))
        grad_pre_rounded = grad_pre.astype(jnp.bfloat16)
        sum_in = sum_in + jnp.dot(normed_block.T, grad_pre_rounded, preferred_element_type=jnp.float32)
        grad_norm = jnp.dot(grad_pre_rounded, w_in.T, preferred_element_type=jnp.float32)
        return ((sum_in, sum_out, sum_bias, sum_scale), (out_block, grad_norm))
    initial = (jnp.zeros((channels, hidden_units), jnp.float32), jnp.zeros((hidden_units, channels), jnp.float32), jnp.zeros((hidden_units,), jnp.float32), jnp.zeros((channels,), jnp.float32))
    stacked = (normed.reshape(-1, block, channels), cotangent.reshape(-1, block, channels), image.reshape(-1, block, channels))
    totals, (out_rows, grad_norm) = lax.scan(block_step, initial, stacked)
    sum_in, sum_out, sum_bias, sum_scale = totals
    out_map = out_rows.reshape(height, breadth, channels)
    grad_norm = grad_norm.reshape(pixels, channels)
    grad_gain = lax.optimization_barrier(jnp.sum(grad_norm * standard, axis=0)) * scale_factor
    scaled = grad_norm * ln_gain
    grad_conv = ((scaled - lax.optimization_barrier(jnp.mean(scaled, axis=1, keepdims=True)) - standard * lax.optimization_barrier(jnp.mean(scaled * standard, axis=1, keepdims=True))) * inverse).astype(jnp.bfloat16)
    grad_conv = grad_conv.reshape(height, breadth, channels)
    flipped = dw_kernel.reshape(channels, KSIZE, KSIZE)[:, ::-1, ::-1].reshape(channels, KSIZE * KSIZE)
    grad_pad = jnp.pad(grad_conv, ((REACH, REACH), (REACH, REACH), (0, 0)))
    grad_back = spatial_stencil(grad_pad, flipped, height, breadth).astype(jnp.bfloat16)
    grad_image = (cotangent.astype(jnp.float32) + grad_back.astype(jnp.float32)).astype(jnp.bfloat16)
    grad_kernel = spatial_taps(padded, grad_conv.astype(jnp.float32), height, breadth) * scale_factor
    return (out_map, grad_image, grad_kernel, sum_in * scale_factor, sum_out * scale_factor, sum_bias * scale_factor, grad_gain, sum_scale * scale_factor)
```

```python
import functools
import math

import jax
import jax.numpy as jnp
from jax import lax
from jax.experimental import pallas as pl
from jax.experimental.pallas import tpu as pltpu
from jax.sharding import PartitionSpec as P

KSIZE = 7
TAPS = KSIZE * KSIZE
DILATE = 2
REACH = 6
LANES = 128
PHASES = 4
EPSILON = 1e-06
VMEM_BYTES = 56 * 1024 * 1024
CONTRACT_ROWS = (((0,), (0,)), ((), ()))
CONTRACT_COLS = (((1,), (1,)), ((), ()))


def dot(left, right, dims=(((1,), (0,)), ((), ()))):
    return lax.dot_general(left, right, dims, preferred_element_type=jnp.float32)


def halo_pad(tile):
    cols = lax.axis_size("col")
    rows = lax.axis_size("row")
    ahead = lambda n: [(i, i + 1) for i in range(n - 1)]
    back = lambda n: [(i + 1, i) for i in range(n - 1)]
    left = lax.ppermute(tile[:, -REACH:], "col", ahead(cols))
    right = lax.ppermute(tile[:, :REACH], "col", back(cols))
    wide = jnp.concatenate([left, tile, right], axis=1)
    top = lax.ppermute(wide[-REACH:], "row", ahead(rows))
    bottom = lax.ppermute(wide[:REACH], "row", back(rows))
    return jnp.concatenate([top, wide, bottom], axis=0)


def spread(source, flat, phased, phase_count):
    flat[...] = source[...].astype(jnp.float32)

    def one_row(row, carry):
        for phase in range(phase_count):
            phased[row, phase] = flat[row, pl.ds(phase, 8, stride=PHASES), :]
        return carry

    lax.fori_loop(0, source.shape[0], one_row, 0)


def stencil_blocks(taps_ref, phased, summed, half_rows):
    def block(index, carry):
        parity = lax.rem(index, 2)
        phase = lax.div(index, 2)
        totals = [jnp.zeros((8, LANES), jnp.float32) for _ in range(half_rows)]
        for tap_col in range(KSIZE):
            weights = [
                jnp.broadcast_to(taps_ref[pl.ds(KSIZE * a + tap_col, 1), :], (8, LANES))
                for a in range(KSIZE)
            ]
            for row in range(half_rows + KSIZE - 1):
                window = phased[parity + 2 * row, phase + DILATE * tap_col]
                for a in range(KSIZE):
                    if 0 <= row - a < half_rows:
                        totals[row - a] = totals[row - a] + weights[a] * window
        for row in range(half_rows):
            summed[parity + 2 * row, pl.ds(phase, 8, stride=PHASES), :] = totals[row]
        return carry

    lax.fori_loop(0, 2 * PHASES, block, 0)


def forward_kernel(padded_ref, taps_ref, out_ref, flat, phased, summed):
    spread(padded_ref, flat, phased, 4 * PHASES)
    stencil_blocks(taps_ref, phased, summed, out_ref.shape[0] // 2)
    out_ref[...] = summed[...].astype(jnp.bfloat16)


def backward_kernel(padded_ref, taps_ref, cot_ref, out_ref, flat, phased, summed):
    spread(padded_ref, flat, phased, 4 * PHASES)
    stencil_blocks(taps_ref, phased, summed, out_ref.shape[0] // 2)
    back = summed[...].astype(jnp.bfloat16).astype(jnp.float32)
    out_ref[...] = (cot_ref[...].astype(jnp.float32) + back).astype(jnp.bfloat16)


def taps_kernel(padded_ref, grad_ref, out_ref, flat, phased, grad_flat, grad_phased, totals):
    half_rows = grad_ref.shape[0] // 2
    spread(padded_ref, flat, phased, 4 * PHASES)
    spread(grad_ref, grad_flat, grad_phased, PHASES)
    totals[...] = jnp.zeros_like(totals)

    def block(index, carry):
        parity = lax.rem(index, 2)
        phase = lax.div(index, 2)
        grads = [grad_phased[parity + 2 * row, phase] for row in range(half_rows)]
        for tap_col in range(KSIZE):
            sums = [totals[KSIZE * a + tap_col] for a in range(KSIZE)]
            for row in range(half_rows + KSIZE - 1):
                window = phased[parity + 2 * row, phase + DILATE * tap_col]
                for a in range(KSIZE):
                    if 0 <= row - a < half_rows:
                        sums[a] = sums[a] + grads[row - a] * window
            for a in range(KSIZE):
                totals[KSIZE * a + tap_col] = sums[a]
        return carry

    lax.fori_loop(0, 2 * PHASES, block, 0)
    out_ref[...] = jnp.sum(totals[...], axis=1)


def stencil_cost(rows, cols, channels):
    return pl.CostEstimate(
        flops=2 * TAPS * rows * cols * channels,
        bytes_accessed=8 * rows * cols * channels,
        transcendentals=0,
    )


def stencil_call(kernel, padded, taps, extra, tile_shape):
    rows, cols, channels = tile_shape
    padded_rows, padded_cols, _ = padded.shape
    field = lambda h, w: pl.BlockSpec((h, w, LANES), lambda c: (0, 0, c))
    return pl.pallas_call(
        kernel,
        grid=(channels // LANES,),
        out_shape=jax.ShapeDtypeStruct(tile_shape, jnp.bfloat16),
        in_specs=[
            field(padded_rows, padded_cols),
            pl.BlockSpec((TAPS, LANES), lambda c: (0, c)),
        ]
        + [field(rows, cols)] * len(extra),
        out_specs=field(rows, cols),
        scratch_shapes=[
            pltpu.VMEM((padded_rows, padded_cols, LANES), jnp.float32),
            pltpu.VMEM((padded_rows, 4 * PHASES, 8, LANES), jnp.float32),
            pltpu.VMEM((rows, cols, LANES), jnp.float32),
        ],
        compiler_params=pltpu.CompilerParams(vmem_limit_bytes=VMEM_BYTES),
        cost_estimate=stencil_cost(rows, cols, channels),
    )(padded, taps, *extra)


def taps_call(padded, grad):
    rows, cols, channels = grad.shape
    padded_rows, padded_cols, _ = padded.shape
    field = lambda h, w: pl.BlockSpec((h, w, LANES), lambda c: (0, 0, c))
    return pl.pallas_call(
        taps_kernel,
        grid=(channels // LANES,),
        out_shape=jax.ShapeDtypeStruct((TAPS, channels), jnp.float32),
        in_specs=[field(padded_rows, padded_cols), field(rows, cols)],
        out_specs=pl.BlockSpec((TAPS, LANES), lambda c: (0, c)),
        scratch_shapes=[
            pltpu.VMEM((padded_rows, padded_cols, LANES), jnp.float32),
            pltpu.VMEM((padded_rows, 4 * PHASES, 8, LANES), jnp.float32),
            pltpu.VMEM((rows, cols, LANES), jnp.float32),
            pltpu.VMEM((rows, PHASES, 8, LANES), jnp.float32),
            pltpu.VMEM((TAPS, 8, LANES), jnp.float32),
        ],
        compiler_params=pltpu.CompilerParams(vmem_limit_bytes=VMEM_BYTES),
        cost_estimate=stencil_cost(rows, cols, channels),
    )(padded, grad)


def standardize(conv):
    values = conv.astype(jnp.float32)
    centered = values - jnp.mean(values, axis=1, keepdims=True)
    inverse = lax.rsqrt(jnp.mean(centered * centered, axis=1, keepdims=True) + EPSILON)
    return centered * inverse, inverse


ROW_TILE = 128


def mlp_kernel(
    conv_ref, image_ref, cot_ref, gain_ref, layer_ref, bias_ref, w_in_ref, w_out_ref,
    out_ref, grad_conv_ref, grad_in_ref, grad_out_ref, bias_sum_ref, gain_sum_ref, scale_sum_ref,
    normed, normed_t, grad_mix, mixed, grad_norm, hidden, grad_pre,
):
    step = pl.program_id(0)
    pixels = normed.shape[0]
    tiles = [pl.ds(start, ROW_TILE) for start in range(0, pixels, ROW_TILE)]

    @pl.when(step == 0)
    def _():
        for tile in tiles:
            standard, _ = standardize(conv_ref[tile, :])
            rounded = (standard * gain_ref[...]).astype(jnp.bfloat16)
            normed[tile, :] = rounded
            normed_t[:, tile] = rounded.T
            grad_mix[tile, :] = (cot_ref[tile, :].astype(jnp.float32) * layer_ref[...]).astype(
                jnp.bfloat16
            )
        mixed[...] = jnp.zeros_like(mixed)
        grad_norm[...] = jnp.zeros_like(grad_norm)

    bias_total = jnp.zeros(bias_sum_ref.shape, jnp.float32)
    for tile in tiles:
        preact = dot(normed[tile, :], w_in_ref[...]) + bias_ref[...]
        grad_hidden = dot(grad_mix[tile, :], w_out_ref[...], CONTRACT_COLS)
        cdf = 0.5 * (1.0 + lax.erf(preact * 0.7071067811865476))
        slope = cdf + preact * jnp.exp(-0.5 * preact * preact) * 0.3989422804014327
        grad_value = grad_hidden * slope
        bias_total = bias_total + jnp.sum(grad_value, axis=0, keepdims=True)
        hidden_tile = (preact * cdf).astype(jnp.bfloat16)
        pre_tile = grad_value.astype(jnp.bfloat16)
        hidden[tile, :] = hidden_tile
        grad_pre[tile, :] = pre_tile
        mixed[tile, :] += dot(hidden_tile, w_out_ref[...])
        grad_norm[tile, :] += dot(pre_tile, w_in_ref[...], CONTRACT_COLS)
    bias_sum_ref[...] = bias_total
    grad_in_ref[...] = dot(normed_t[...], grad_pre[...]).astype(grad_in_ref.dtype)
    grad_out_ref[...] = dot(hidden[...], grad_mix[...], CONTRACT_ROWS).astype(grad_out_ref.dtype)

    @pl.when(step == pl.num_programs(0) - 1)
    def _():
        gain_total = jnp.zeros(gain_sum_ref.shape, jnp.float32)
        scale_total = jnp.zeros(scale_sum_ref.shape, jnp.float32)
        for tile in tiles:
            mix = mixed[tile, :]
            out_ref[tile, :] = (
                image_ref[tile, :].astype(jnp.float32) + layer_ref[...] * mix
            ).astype(jnp.bfloat16)
            scale_total = scale_total + jnp.sum(
                cot_ref[tile, :].astype(jnp.float32) * mix, axis=0, keepdims=True
            )
            standard, inverse = standardize(conv_ref[tile, :])
            grad = grad_norm[tile, :]
            gain_total = gain_total + jnp.sum(grad * standard, axis=0, keepdims=True)
            scaled = grad * gain_ref[...]
            grad_conv_ref[tile, :] = (
                (
                    scaled
                    - jnp.mean(scaled, axis=1, keepdims=True)
                    - standard * jnp.mean(scaled * standard, axis=1, keepdims=True)
                )
                * inverse
            ).astype(jnp.bfloat16)
        gain_sum_ref[...] = gain_total
        scale_sum_ref[...] = scale_total


def mlp_call(conv, image, cot, gain, layer, bias, w_in, w_out, grad_type, chunk=256):
    pixels, channels = conv.shape
    hidden_units = w_in.shape[1]
    whole = lambda h, w: pl.BlockSpec((h, w), lambda s: (0, 0))
    f32 = lambda *shape: jax.ShapeDtypeStruct(shape, jnp.float32)
    bf16 = lambda *shape: jax.ShapeDtypeStruct(shape, jnp.bfloat16)
    return pl.pallas_call(
        mlp_kernel,
        grid=(hidden_units // chunk,),
        out_shape=(
            bf16(pixels, channels),
            bf16(pixels, channels),
            jax.ShapeDtypeStruct((channels, hidden_units), grad_type),
            jax.ShapeDtypeStruct((hidden_units, channels), grad_type),
            f32(1, hidden_units),
            f32(1, channels),
            f32(1, channels),
        ),
        in_specs=[
            whole(pixels, channels),
            whole(pixels, channels),
            whole(pixels, channels),
            whole(1, channels),
            whole(1, channels),
            pl.BlockSpec((1, chunk), lambda s: (0, s)),
            pl.BlockSpec((channels, chunk), lambda s: (0, s)),
            pl.BlockSpec((chunk, channels), lambda s: (s, 0)),
        ],
        out_specs=(
            whole(pixels, channels),
            whole(pixels, channels),
            pl.BlockSpec((channels, chunk), lambda s: (0, s)),
            pl.BlockSpec((chunk, channels), lambda s: (s, 0)),
            pl.BlockSpec((1, chunk), lambda s: (0, s)),
            whole(1, channels),
            whole(1, channels),
        ),
        scratch_shapes=[
            pltpu.VMEM((pixels, channels), jnp.bfloat16),
            pltpu.VMEM((channels, pixels), jnp.bfloat16),
            pltpu.VMEM((pixels, channels), jnp.bfloat16),
            pltpu.VMEM((pixels, channels), jnp.float32),
            pltpu.VMEM((pixels, channels), jnp.float32),
            pltpu.VMEM((pixels, chunk), jnp.bfloat16),
            pltpu.VMEM((pixels, chunk), jnp.bfloat16),
        ],
        compiler_params=pltpu.CompilerParams(vmem_limit_bytes=VMEM_BYTES),
        cost_estimate=pl.CostEstimate(
            flops=12 * pixels * channels * hidden_units,
            bytes_accessed=12 * channels * hidden_units,
            transcendentals=2 * pixels * hidden_units,
        ),
    )(conv, image, cot, gain, layer, bias, w_in, w_out)


def local(image, dw_kernel, ln_gain, w_in, b_in, w_out, layer_scale, cotangent):
    tile_shape = image.shape
    tile_rows, tile_cols, channels = tile_shape
    group_count = lax.axis_size("row") * lax.axis_size("col")
    pixels = tile_rows * tile_cols
    scale_factor = 1.0 / math.sqrt(pixels * group_count)
    flat = lambda field: field.reshape(pixels, channels)
    full_in = lax.all_gather(w_in, "col", axis=0, tiled=True)
    full_out = lax.all_gather(w_out, "col", axis=0, tiled=True)
    taps = dw_kernel.T
    padded = halo_pad(image)
    conv = stencil_call(forward_kernel, padded, taps, (), tile_shape)
    out_map, grad_conv, grad_in, grad_out, bias_part, gain_part, scale_part = mlp_call(
        flat(conv),
        flat(image),
        flat(cotangent),
        ln_gain[None],
        layer_scale[None],
        b_in[None],
        full_in,
        full_out,
        jnp.float32,
    )
    part_in = lax.psum_scatter(grad_in, "col", scatter_dimension=0, tiled=True)
    part_out = lax.psum_scatter(grad_out, "col", scatter_dimension=0, tiled=True)
    grad_conv = grad_conv.reshape(tile_shape)
    grad_padded = halo_pad(grad_conv)
    tap_part = taps_call(padded, grad_conv)
    grad_image = stencil_call(backward_kernel, grad_padded, taps[::-1], (cotangent,), tile_shape)
    summed_in, summed_out = lax.psum((part_in, part_out), "row")
    scale_sum, bias_sum, gain_sum, tap_sum = lax.psum(
        (scale_part[0], bias_part[0], gain_part[0], tap_part), ("row", "col")
    )
    group_size = channels // group_count
    group_index = lax.axis_index("row") * lax.axis_size("col") + lax.axis_index("col")
    grad_kernel = lax.dynamic_slice_in_dim(tap_sum.T, group_index * group_size, group_size, 0)
    return (
        out_map.reshape(tile_shape),
        grad_image,
        grad_kernel * scale_factor,
        summed_in * scale_factor,
        summed_out * scale_factor,
        bias_sum * scale_factor,
        gain_sum * scale_factor,
        scale_sum * scale_factor,
    )


def solution(mesh):
    in_specs = (
        P("row", "col", None),
        P(),
        P(),
        P("col", None),
        P(),
        P("col", None),
        P(),
        P("row", "col", None),
    )
    out_specs = (
        P("row", "col", None),
        P("row", "col", None),
        P(("row", "col"), None),
        P("col", None),
        P("col", None),
        P(),
        P(),
        P(),
    )
    return jax.shard_map(local, mesh=mesh, in_specs=in_specs, out_specs=out_specs, check_vma=False)
```

```python
import functools
import math

import jax
import jax.numpy as jnp
from jax import lax
from jax.experimental import pallas as pl
from jax.experimental.pallas import tpu as pltpu
from jax.sharding import PartitionSpec as P

KSIZE = 7
TAPS = KSIZE * KSIZE
DILATE = 2
REACH = 6
LANES = 128
PHASES = 4
EPSILON = 1e-06
VMEM_BYTES = 56 * 1024 * 1024
CONTRACT_ROWS = (((0,), (0,)), ((), ()))
CONTRACT_COLS = (((1,), (1,)), ((), ()))


def dot(left, right, dims=(((1,), (0,)), ((), ()))):
    return lax.dot_general(left, right, dims, preferred_element_type=jnp.float32)


def halo_pad(tile):
    cols = lax.axis_size("col")
    rows = lax.axis_size("row")
    ahead = lambda n: [(i, i + 1) for i in range(n - 1)]
    back = lambda n: [(i + 1, i) for i in range(n - 1)]
    left = lax.ppermute(tile[:, -REACH:], "col", ahead(cols))
    right = lax.ppermute(tile[:, :REACH], "col", back(cols))
    wide = jnp.concatenate([left, tile, right], axis=1)
    top = lax.ppermute(wide[-REACH:], "row", ahead(rows))
    bottom = lax.ppermute(wide[:REACH], "row", back(rows))
    return jnp.concatenate([top, wide, bottom], axis=0)


def spread(source, flat, phased, phase_count):
    flat[...] = source[...].astype(jnp.float32)

    def one_row(row, carry):
        for phase in range(phase_count):
            phased[row, phase] = flat[row, pl.ds(phase, 8, stride=PHASES), :]
        return carry

    lax.fori_loop(0, source.shape[0], one_row, 0)


def stencil_blocks(taps_ref, phased, summed, half_rows):
    def block(index, carry):
        parity = lax.rem(index, 2)
        phase = lax.div(index, 2)
        totals = [jnp.zeros((8, LANES), jnp.float32) for _ in range(half_rows)]
        for tap_col in range(KSIZE):
            weights = [
                jnp.broadcast_to(taps_ref[pl.ds(KSIZE * a + tap_col, 1), :], (8, LANES))
                for a in range(KSIZE)
            ]
            for row in range(half_rows + KSIZE - 1):
                window = phased[parity + 2 * row, phase + DILATE * tap_col]
                for a in range(KSIZE):
                    if 0 <= row - a < half_rows:
                        totals[row - a] = totals[row - a] + weights[a] * window
        for row in range(half_rows):
            summed[parity + 2 * row, pl.ds(phase, 8, stride=PHASES), :] = totals[row]
        return carry

    lax.fori_loop(0, 2 * PHASES, block, 0)


def forward_kernel(padded_ref, taps_ref, out_ref, flat, phased, summed):
    spread(padded_ref, flat, phased, 4 * PHASES)
    stencil_blocks(taps_ref, phased, summed, out_ref.shape[0] // 2)
    out_ref[...] = summed[...].astype(jnp.bfloat16)


def backward_kernel(padded_ref, taps_ref, cot_ref, out_ref, flat, phased, summed):
    spread(padded_ref, flat, phased, 4 * PHASES)
    stencil_blocks(taps_ref, phased, summed, out_ref.shape[0] // 2)
    back = summed[...].astype(jnp.bfloat16).astype(jnp.float32)
    out_ref[...] = (cot_ref[...].astype(jnp.float32) + back).astype(jnp.bfloat16)


def taps_kernel(padded_ref, grad_ref, out_ref, flat, phased, grad_flat, grad_phased, totals):
    half_rows = grad_ref.shape[0] // 2
    spread(padded_ref, flat, phased, 4 * PHASES)
    spread(grad_ref, grad_flat, grad_phased, PHASES)
    totals[...] = jnp.zeros_like(totals)

    def block(index, carry):
        parity = lax.rem(index, 2)
        phase = lax.div(index, 2)
        grads = [grad_phased[parity + 2 * row, phase] for row in range(half_rows)]
        for tap_col in range(KSIZE):
            sums = [totals[KSIZE * a + tap_col] for a in range(KSIZE)]
            for row in range(half_rows + KSIZE - 1):
                window = phased[parity + 2 * row, phase + DILATE * tap_col]
                for a in range(KSIZE):
                    if 0 <= row - a < half_rows:
                        sums[a] = sums[a] + grads[row - a] * window
            for a in range(KSIZE):
                totals[KSIZE * a + tap_col] = sums[a]
        return carry

    lax.fori_loop(0, 2 * PHASES, block, 0)
    out_ref[...] = jnp.sum(totals[...], axis=1)


def stencil_cost(rows, cols, channels):
    return pl.CostEstimate(
        flops=2 * TAPS * rows * cols * channels,
        bytes_accessed=8 * rows * cols * channels,
        transcendentals=0,
    )


def stencil_call(kernel, padded, taps, extra, tile_shape):
    rows, cols, channels = tile_shape
    padded_rows, padded_cols, _ = padded.shape
    field = lambda h, w: pl.BlockSpec((h, w, LANES), lambda c: (0, 0, c))
    return pl.pallas_call(
        kernel,
        grid=(channels // LANES,),
        out_shape=jax.ShapeDtypeStruct(tile_shape, jnp.bfloat16),
        in_specs=[
            field(padded_rows, padded_cols),
            pl.BlockSpec((TAPS, LANES), lambda c: (0, c)),
        ]
        + [field(rows, cols)] * len(extra),
        out_specs=field(rows, cols),
        scratch_shapes=[
            pltpu.VMEM((padded_rows, padded_cols, LANES), jnp.float32),
            pltpu.VMEM((padded_rows, 4 * PHASES, 8, LANES), jnp.float32),
            pltpu.VMEM((rows, cols, LANES), jnp.float32),
        ],
        compiler_params=pltpu.CompilerParams(vmem_limit_bytes=VMEM_BYTES),
        cost_estimate=stencil_cost(rows, cols, channels),
    )(padded, taps, *extra)


def taps_call(padded, grad):
    rows, cols, channels = grad.shape
    padded_rows, padded_cols, _ = padded.shape
    field = lambda h, w: pl.BlockSpec((h, w, LANES), lambda c: (0, 0, c))
    return pl.pallas_call(
        taps_kernel,
        grid=(channels // LANES,),
        out_shape=jax.ShapeDtypeStruct((TAPS, channels), jnp.float32),
        in_specs=[field(padded_rows, padded_cols), field(rows, cols)],
        out_specs=pl.BlockSpec((TAPS, LANES), lambda c: (0, c)),
        scratch_shapes=[
            pltpu.VMEM((padded_rows, padded_cols, LANES), jnp.float32),
            pltpu.VMEM((padded_rows, 4 * PHASES, 8, LANES), jnp.float32),
            pltpu.VMEM((rows, cols, LANES), jnp.float32),
            pltpu.VMEM((rows, PHASES, 8, LANES), jnp.float32),
            pltpu.VMEM((TAPS, 8, LANES), jnp.float32),
        ],
        compiler_params=pltpu.CompilerParams(vmem_limit_bytes=VMEM_BYTES),
        cost_estimate=stencil_cost(rows, cols, channels),
    )(padded, grad)


def standardize(conv):
    values = conv.astype(jnp.float32)
    centered = values - jnp.mean(values, axis=1, keepdims=True)
    inverse = lax.rsqrt(jnp.mean(centered * centered, axis=1, keepdims=True) + EPSILON)
    return centered * inverse, inverse


ROW_TILE = 128


def mlp_kernel(
    conv_ref, image_ref, cot_ref, gain_ref, layer_ref, bias_ref, w_in_ref, w_out_ref,
    out_ref, grad_conv_ref, grad_in_ref, grad_out_ref, bias_sum_ref, gain_sum_ref, scale_sum_ref,
    normed, normed_t, grad_mix, mixed, grad_norm, hidden, grad_pre,
):
    step = pl.program_id(0)
    pixels = normed.shape[0]
    tiles = [pl.ds(start, ROW_TILE) for start in range(0, pixels, ROW_TILE)]

    @pl.when(step == 0)
    def _():
        for tile in tiles:
            standard, _ = standardize(conv_ref[tile, :])
            rounded = (standard * gain_ref[...]).astype(jnp.bfloat16)
            normed[tile, :] = rounded
            normed_t[:, tile] = rounded.T
            grad_mix[tile, :] = (cot_ref[tile, :].astype(jnp.float32) * layer_ref[...]).astype(
                jnp.bfloat16
            )
        mixed[...] = jnp.zeros_like(mixed)
        grad_norm[...] = jnp.zeros_like(grad_norm)

    bias_total = jnp.zeros(bias_sum_ref.shape, jnp.float32)
    for tile in tiles:
        preact = dot(normed[tile, :], w_in_ref[...]) + bias_ref[...]
        grad_hidden = dot(grad_mix[tile, :], w_out_ref[...], CONTRACT_COLS)
        cdf = 0.5 * (1.0 + lax.erf(preact * 0.7071067811865476))
        slope = cdf + preact * jnp.exp(-0.5 * preact * preact) * 0.3989422804014327
        grad_value = grad_hidden * slope
        bias_total = bias_total + jnp.sum(grad_value, axis=0, keepdims=True)
        hidden_tile = (preact * cdf).astype(jnp.bfloat16)
        pre_tile = grad_value.astype(jnp.bfloat16)
        hidden[tile, :] = hidden_tile
        grad_pre[tile, :] = pre_tile
        mixed[tile, :] += dot(hidden_tile, w_out_ref[...])
        grad_norm[tile, :] += dot(pre_tile, w_in_ref[...], CONTRACT_COLS)
    bias_sum_ref[...] = bias_total
    grad_in_ref[...] = dot(normed_t[...], grad_pre[...]).astype(grad_in_ref.dtype)
    grad_out_ref[...] = dot(hidden[...], grad_mix[...], CONTRACT_ROWS).astype(grad_out_ref.dtype)

    @pl.when(step == pl.num_programs(0) - 1)
    def _():
        gain_total = jnp.zeros(gain_sum_ref.shape, jnp.float32)
        scale_total = jnp.zeros(scale_sum_ref.shape, jnp.float32)
        for tile in tiles:
            mix = mixed[tile, :]
            out_ref[tile, :] = (
                image_ref[tile, :].astype(jnp.float32) + layer_ref[...] * mix
            ).astype(jnp.bfloat16)
            scale_total = scale_total + jnp.sum(
                cot_ref[tile, :].astype(jnp.float32) * mix, axis=0, keepdims=True
            )
            standard, inverse = standardize(conv_ref[tile, :])
            grad = grad_norm[tile, :]
            gain_total = gain_total + jnp.sum(grad * standard, axis=0, keepdims=True)
            scaled = grad * gain_ref[...]
            grad_conv_ref[tile, :] = (
                (
                    scaled
                    - jnp.mean(scaled, axis=1, keepdims=True)
                    - standard * jnp.mean(scaled * standard, axis=1, keepdims=True)
                )
                * inverse
            ).astype(jnp.bfloat16)
        gain_sum_ref[...] = gain_total
        scale_sum_ref[...] = scale_total


def mlp_call(conv, image, cot, gain, layer, bias, w_in, w_out, grad_type, chunk=256):
    pixels, channels = conv.shape
    hidden_units = w_out.shape[0]
    quarter_steps = hidden_units // (4 * chunk)
    quartered = pl.BlockSpec(
        (None, channels, chunk), lambda s: (s // quarter_steps, 0, s % quarter_steps)
    )
    whole = lambda h, w: pl.BlockSpec((h, w), lambda s: (0, 0))
    f32 = lambda *shape: jax.ShapeDtypeStruct(shape, jnp.float32)
    bf16 = lambda *shape: jax.ShapeDtypeStruct(shape, jnp.bfloat16)
    return pl.pallas_call(
        mlp_kernel,
        grid=(hidden_units // chunk,),
        out_shape=(
            bf16(pixels, channels),
            bf16(pixels, channels),
            jax.ShapeDtypeStruct((4, channels, hidden_units // 4), grad_type),
            jax.ShapeDtypeStruct((hidden_units, channels), grad_type),
            f32(1, hidden_units),
            f32(1, channels),
            f32(1, channels),
        ),
        in_specs=[
            whole(pixels, channels),
            whole(pixels, channels),
            whole(pixels, channels),
            whole(1, channels),
            whole(1, channels),
            pl.BlockSpec((1, chunk), lambda s: (0, s)),
            quartered,
            pl.BlockSpec((chunk, channels), lambda s: (s, 0)),
        ],
        out_specs=(
            whole(pixels, channels),
            whole(pixels, channels),
            quartered,
            pl.BlockSpec((chunk, channels), lambda s: (s, 0)),
            pl.BlockSpec((1, chunk), lambda s: (0, s)),
            whole(1, channels),
            whole(1, channels),
        ),
        scratch_shapes=[
            pltpu.VMEM((pixels, channels), jnp.bfloat16),
            pltpu.VMEM((channels, pixels), jnp.bfloat16),
            pltpu.VMEM((pixels, channels), jnp.bfloat16),
            pltpu.VMEM((pixels, channels), jnp.float32),
            pltpu.VMEM((pixels, channels), jnp.float32),
            pltpu.VMEM((pixels, chunk), jnp.bfloat16),
            pltpu.VMEM((pixels, chunk), jnp.bfloat16),
        ],
        compiler_params=pltpu.CompilerParams(vmem_limit_bytes=VMEM_BYTES),
        cost_estimate=pl.CostEstimate(
            flops=12 * pixels * channels * hidden_units,
            bytes_accessed=12 * channels * hidden_units,
            transcendentals=2 * pixels * hidden_units,
        ),
    )(conv, image, cot, gain, layer, bias, w_in, w_out)


MESH = pl.DeviceIdType.MESH
PARTS = 2


class Place:
    def __init__(self):
        self.row = lax.axis_index("row")
        self.col = lax.axis_index("col")
        self.depth = lax.axis_size("col") // 4
        self.z = self.col // 4
        self.y = (self.col // 2) % 2
        self.x = self.col % 2
        self.core = self.row % 2

    def at(self, z, y, x):
        return (self.row, 4 * z + 2 * y + x)

    def z_peer(self, hop):
        return self.at((self.z + hop) % self.depth, self.y, self.x)

    def y_peer(self):
        return self.at(self.z, 1 - self.y, self.x)

    def x_peer(self):
        return self.at(self.z, self.y, 1 - self.x)

    def core_peer(self):
        return (self.row + 1 - 2 * self.core, self.col)

    def greet(self):
        barrier = pltpu.get_barrier_semaphore()
        peers = [self.z_peer(hop) for hop in range(1, self.depth)]
        peers += [self.y_peer(), self.x_peer(), self.core_peer()]
        for peer in peers:
            pl.semaphore_signal(barrier, inc=1, device_id=peer, device_id_type=MESH)
        pl.semaphore_wait(barrier, len(peers))


class Mail:
    def __init__(self, send_sems, recv_sems):
        self.send_sems, self.recv_sems, self.copies = send_sems, recv_sems, []

    def send(self, source, target, peer):
        slot = len(self.copies)
        copy = pltpu.make_async_remote_copy(
            src_ref=source,
            dst_ref=target,
            send_sem=self.send_sems.at[slot],
            recv_sem=self.recv_sems.at[slot],
            device_id=peer,
            device_id_type=MESH,
        )
        copy.start()
        self.copies.append(copy)
        return copy

    def finish(self):
        for copy in self.copies:
            copy.wait_send()


def gather_kernel(shard_in, shard_out, full_in, full_out, send_sems, recv_sems, own_sems):
    place = Place()
    z, y, x = place.z, place.y, place.x
    mine = pl.ds(2 * place.core, 2)
    own_in = pltpu.make_async_copy(shard_in.at[mine], full_in.at[mine, z, y, x], own_sems.at[0])
    own_out = pltpu.make_async_copy(
        shard_out.at[mine], full_out.at[z, y, x, mine], own_sems.at[1]
    )
    own_in.start()
    own_out.start()
    place.greet()
    own_in.wait()
    own_out.wait()
    mail = Mail(send_sems, recv_sems)
    every = slice(None)

    def view(array, quarter, zs, ys, xs):
        if array == 0:
            return full_in.at[quarter, zs, ys, xs]
        return full_out.at[zs, ys, xs, quarter]

    def send(piece, stage):
        array, part = piece
        quarter = 2 * place.core + part
        first_y = part == 0
        if stage == 0:
            block = view(array, quarter, z, y, x)
            return [mail.send(block, block, place.z_peer(hop)) for hop in range(1, place.depth)]
        if stage == 1:
            block = view(array, quarter, every, y, x)
            return [mail.send(block, block, place.y_peer() if first_y else place.x_peer())]
        if stage == 2:
            block = view(array, quarter, every, *((every, x) if first_y else (y, every)))
            return [mail.send(block, block, place.x_peer() if first_y else place.y_peer())]
        block = view(array, quarter, every, every, every)
        return [mail.send(block, block, place.core_peer())]

    pieces = [(array, part) for array in range(2) for part in range(PARTS)]
    flying = [[] for _ in pieces]
    for tick in range(len(pieces) + 4):
        for index in range(len(pieces) - 1, -1, -1):
            stage = tick - index
            if 0 <= stage <= 4:
                for copy in flying[index]:
                    copy.wait_recv()
                if stage < 4:
                    flying[index] = send(pieces[index], stage)
    mail.finish()


def gather_call(w_in, w_out):
    depth = lax.axis_size("col") // 4
    in_rows, hidden_units = w_in.shape
    out_rows, channels = w_out.shape
    width, height = hidden_units // 4, out_rows // 4
    shard_in = w_in.reshape(in_rows, 4, width).transpose(1, 0, 2)
    shard_out = w_out.reshape(4, height, channels)
    copies = 4 * (depth - 1 + 3)
    anywhere = pl.BlockSpec(memory_space=pl.ANY)
    full_in, full_out = pl.pallas_call(
        gather_kernel,
        out_shape=(
            jax.ShapeDtypeStruct((4, depth, 2, 2, in_rows, width), w_in.dtype),
            jax.ShapeDtypeStruct((depth, 2, 2, 4, height, channels), w_out.dtype),
        ),
        in_specs=[anywhere, anywhere],
        out_specs=(anywhere, anywhere),
        scratch_shapes=[
            pltpu.SemaphoreType.DMA((copies,)),
            pltpu.SemaphoreType.DMA((copies,)),
            pltpu.SemaphoreType.DMA((2,)),
        ],
        compiler_params=pltpu.CompilerParams(
            collective_id=0, has_side_effects=True, vmem_limit_bytes=VMEM_BYTES
        ),
    )(shard_in, shard_out)
    return full_in.reshape(4, 4 * depth * in_rows, width), full_out.reshape(-1, channels)


def scatter_kernel(
    grad_in, grad_out, small, total, small_total,
    recv_core, sum_core, recv_one, sum_one, recv_two, sum_two, recv_z, small_pair, small_z,
    send_sems, recv_sems,
):
    place = Place()
    z, y, x = place.z, place.y, place.x
    depth = place.depth
    place.greet()
    mail = Mail(send_sems, recv_sems)
    f32 = jnp.float32
    every = slice(None)

    def block_of(array, quarter, zz, yy, xx):
        if array == 0:
            return grad_in.at[quarter, zz, yy, xx]
        return grad_out.at[zz, yy, xx, quarter]

    pieces = [(array, part) for array in range(2) for part in range(PARTS)]
    small_copy = mail.send(small, small_pair.at[0], place.core_peer())
    flying = []
    for index, (array, part) in enumerate(pieces):
        source = block_of(array, 2 * (1 - place.core) + part, every, every, every)
        flying.append([mail.send(source, recv_core.at[index], place.core_peer())])

    def add(target, left, right):
        target[...] = (left[...].astype(f32) + right[...].astype(f32)).astype(target.dtype)

    def advance(index, stage):
        array, part = pieces[index]
        quarter = 2 * place.core + part
        x_first = part == 0
        near, far = (x, y) if x_first else (y, x)
        near_peer, far_peer = place.x_peer(), place.y_peer()
        if not x_first:
            near_peer, far_peer = far_peer, near_peer
        for copy in flying[index]:
            copy.wait_recv()
        if stage == 0:

            def add_core(zz, carry):
                for yy in range(2):
                    for xx in range(2):
                        first, second = (xx, yy) if x_first else (yy, xx)
                        add(
                            sum_core.at[index, first, zz, second],
                            block_of(array, quarter, zz, yy, xx),
                            recv_core.at[index, zz, yy, xx],
                        )
                return carry

            lax.fori_loop(0, depth, add_core, 0)
            return [mail.send(sum_core.at[index, 1 - near], recv_one.at[index], near_peer)]
        if stage == 1:

            def add_one(zz, carry):
                for second in range(2):
                    add(
                        sum_one.at[index, second, zz],
                        sum_core.at[index, near, zz, second],
                        recv_one.at[index, zz, second],
                    )
                return carry

            lax.fori_loop(0, depth, add_one, 0)
            return [mail.send(sum_one.at[index, 1 - far], recv_two.at[index], far_peer)]
        if stage == 2:

            def add_two(zz, carry):
                add(
                    sum_two.at[index, zz],
                    sum_one.at[index, far, zz],
                    recv_two.at[index, zz],
                )
                return carry

            lax.fori_loop(0, depth, add_two, 0)
            return [
                mail.send(
                    sum_two.at[index, (z + hop) % depth],
                    recv_z.at[index, hop - 1],
                    place.z_peer(hop),
                )
                for hop in range(1, depth)
            ]
        if stage == 3:
            owned = sum_two[index, z].astype(f32)
            for hop in range(1, depth):
                owned = owned + recv_z[index, hop - 1].astype(f32)
            total[array, quarter] = owned
            block = total.at[array, quarter]
            return [mail.send(block, block, place.core_peer())]
        return []

    def advance_small(stage):
        if stage < 3:
            small_flying[0].wait_recv()
            source = small if stage == 0 else small_pair.at[2 + stage]
            if stage < 2:
                add(small_pair.at[3 + stage], source, small_pair.at[stage])
                peer = place.x_peer() if stage == 0 else place.y_peer()
                return [mail.send(small_pair.at[3 + stage], small_pair.at[1 + stage], peer)]
            add(small_z.at[0], source, small_pair.at[stage])
            return [
                mail.send(small_z.at[0], small_z.at[hop], place.z_peer(hop))
                for hop in range(1, depth)
            ]
        for copy in small_flying:
            copy.wait_recv()
        summed = small_z[z]
        for other in range(1, depth):
            summed = summed + small_z[(z + depth - other) % depth]
        small_total[...] = summed
        return []

    small_flying = [small_copy]
    for tick in range(len(pieces) + 4):
        for index in range(len(pieces) - 1, -1, -1):
            if 0 <= tick - index <= 4:
                flying[index] = advance(index, tick - index)
        if tick < 4:
            small_flying = advance_small(tick)
    mail.finish()


def scatter_call(grad_in, grad_out, small):
    depth = lax.axis_size("col") // 4
    _, channels, width = grad_in.shape
    height = channels // (4 * depth)
    grad_in = grad_in.reshape(4, depth, 2, 2, height, width)
    grad_out = grad_out.reshape(depth, 2, 2, 4, -1, channels)
    assert grad_out.shape[4:] == (height, width)
    kind = grad_in.dtype
    vmem = pl.BlockSpec(memory_space=pltpu.VMEM)
    copies = 4 * (1 + 1 + 1 + depth - 1 + 1) + 3 + depth - 1
    return pl.pallas_call(
        scatter_kernel,
        out_shape=(
            jax.ShapeDtypeStruct((2, 4, height, width), jnp.float32),
            jax.ShapeDtypeStruct(small.shape, jnp.float32),
        ),
        in_specs=[vmem] * 3,
        out_specs=(vmem, vmem),
        scratch_shapes=[
            pltpu.VMEM((4, depth, 2, 2, height, width), kind),
            pltpu.VMEM((4, 2, depth, 2, height, width), kind),
            pltpu.VMEM((4, depth, 2, height, width), kind),
            pltpu.VMEM((4, 2, depth, height, width), kind),
            pltpu.VMEM((4, depth, height, width), kind),
            pltpu.VMEM((4, depth, height, width), kind),
            pltpu.VMEM((4, depth - 1, height, width), kind),
            pltpu.VMEM((5,) + small.shape, jnp.float32),
            pltpu.VMEM((depth,) + small.shape, jnp.float32),
            pltpu.SemaphoreType.DMA((copies,)),
            pltpu.SemaphoreType.DMA((copies,)),
        ],
        compiler_params=pltpu.CompilerParams(
            collective_id=1, has_side_effects=True, vmem_limit_bytes=VMEM_BYTES
        ),
    )(grad_in, grad_out, small)


def local(image, dw_kernel, ln_gain, w_in, b_in, w_out, layer_scale, cotangent):
    tile_shape = image.shape
    tile_rows, tile_cols, channels = tile_shape
    group_count = lax.axis_size("row") * lax.axis_size("col")
    pixels = tile_rows * tile_cols
    scale_factor = 1.0 / math.sqrt(pixels * group_count)
    flat = lambda field: field.reshape(pixels, channels)
    full_in, full_out = gather_call(w_in, w_out)
    taps = dw_kernel.T
    padded = halo_pad(image)
    conv = stencil_call(forward_kernel, padded, taps, (), tile_shape)
    out_map, grad_conv, grad_in, grad_out, bias_part, gain_part, scale_part = mlp_call(
        flat(conv),
        flat(image),
        flat(cotangent),
        ln_gain[None],
        layer_scale[None],
        b_in[None],
        full_in,
        full_out,
        jnp.bfloat16,
    )
    grad_conv = grad_conv.reshape(tile_shape)
    grad_padded = halo_pad(grad_conv)
    tap_part = taps_call(padded, grad_conv)
    grad_image = stencil_call(backward_kernel, grad_padded, taps[::-1], (cotangent,), tile_shape)
    small_rows = [tap_part, bias_part.reshape(-1, channels), gain_part, scale_part]
    small = jnp.concatenate(small_rows, axis=0)
    small = jnp.pad(small, ((0, -small.shape[0] % 8), (0, 0)))
    total, small_total = scatter_call(grad_in, grad_out, small)
    if lax.axis_size("row") > 2:
        total, small_total = (0.5 * field for field in lax.psum((total, small_total), "row"))
    summed_in = total[0].transpose(1, 0, 2).reshape(w_in.shape)
    summed_out = total[1].reshape(w_out.shape)
    tap_sum = small_total[:TAPS]
    rows_used = TAPS + bias_part.size // channels
    bias_sum = small_total[TAPS:rows_used].reshape(-1)
    gain_sum, scale_sum = small_total[rows_used], small_total[rows_used + 1]
    group_size = channels // group_count
    group_index = lax.axis_index("row") * lax.axis_size("col") + lax.axis_index("col")
    grad_kernel = lax.dynamic_slice_in_dim(tap_sum.T, group_index * group_size, group_size, 0)
    return (
        out_map.reshape(tile_shape),
        grad_image,
        grad_kernel * scale_factor,
        summed_in * scale_factor,
        summed_out * scale_factor,
        bias_sum * scale_factor,
        gain_sum * scale_factor,
        scale_sum * scale_factor,
    )


def solution(mesh):
    in_specs = (
        P("row", "col", None),
        P(),
        P(),
        P("col", None),
        P(),
        P("col", None),
        P(),
        P("row", "col", None),
    )
    out_specs = (
        P("row", "col", None),
        P("row", "col", None),
        P(("row", "col"), None),
        P("col", None),
        P("col", None),
        P(),
        P(),
        P(),
    )
    return jax.shard_map(local, mesh=mesh, in_specs=in_specs, out_specs=out_specs, check_vma=False)
```

```python
import functools
import math

import jax
import jax.numpy as jnp
from jax import lax
from jax.experimental import pallas as pl
from jax.experimental.pallas import tpu as pltpu
from jax.sharding import PartitionSpec as P

KSIZE = 7
TAPS = KSIZE * KSIZE
DILATE = 2
REACH = 6
LANES = 128
PHASES = 4
EPSILON = 1e-06
VMEM_BYTES = 56 * 1024 * 1024
CONTRACT_ROWS = (((0,), (0,)), ((), ()))
CONTRACT_COLS = (((1,), (1,)), ((), ()))


def dot(left, right, dims=(((1,), (0,)), ((), ()))):
    return lax.dot_general(left, right, dims, preferred_element_type=jnp.float32)


def halo_pad(tile):
    cols = lax.axis_size("col")
    rows = lax.axis_size("row")
    ahead = lambda n: [(i, i + 1) for i in range(n - 1)]
    back = lambda n: [(i + 1, i) for i in range(n - 1)]
    left = lax.ppermute(tile[:, -REACH:], "col", ahead(cols))
    right = lax.ppermute(tile[:, :REACH], "col", back(cols))
    wide = jnp.concatenate([left, tile, right], axis=1)
    top = lax.ppermute(wide[-REACH:], "row", ahead(rows))
    bottom = lax.ppermute(wide[:REACH], "row", back(rows))
    return jnp.concatenate([top, wide, bottom], axis=0)


def spread(source, flat, phased, phase_count):
    flat[...] = source[...].astype(jnp.float32)

    def one_row(row, carry):
        for phase in range(phase_count):
            phased[row, phase] = flat[row, pl.ds(phase, 8, stride=PHASES), :]
        return carry

    lax.fori_loop(0, source.shape[0], one_row, 0)


def stencil_blocks(taps_ref, phased, summed, half_rows):
    def block(index, carry):
        parity = lax.rem(index, 2)
        phase = lax.div(index, 2)
        totals = [jnp.zeros((8, LANES), jnp.float32) for _ in range(half_rows)]
        for tap_col in range(KSIZE):
            weights = [
                jnp.broadcast_to(taps_ref[pl.ds(KSIZE * a + tap_col, 1), :], (8, LANES))
                for a in range(KSIZE)
            ]
            for row in range(half_rows + KSIZE - 1):
                window = phased[parity + 2 * row, phase + DILATE * tap_col]
                for a in range(KSIZE):
                    if 0 <= row - a < half_rows:
                        totals[row - a] = totals[row - a] + weights[a] * window
        for row in range(half_rows):
            summed[parity + 2 * row, pl.ds(phase, 8, stride=PHASES), :] = totals[row]
        return carry

    lax.fori_loop(0, 2 * PHASES, block, 0)


def forward_block(padded_ref, taps_ref, out_ref, flat, phased, summed):
    spread(padded_ref, flat, phased, 4 * PHASES)
    stencil_blocks(taps_ref, phased, summed, out_ref.shape[0] // 2)
    out_ref[...] = summed[...].astype(jnp.bfloat16)


def backward_kernel(padded_ref, taps_ref, cot_ref, out_ref, flat, phased, summed):
    spread(padded_ref, flat, phased, 4 * PHASES)
    stencil_blocks(taps_ref, phased, summed, out_ref.shape[0] // 2)
    back = summed[...].astype(jnp.bfloat16).astype(jnp.float32)
    out_ref[...] = (cot_ref[...].astype(jnp.float32) + back).astype(jnp.bfloat16)


def taps_kernel(padded_ref, grad_ref, out_ref, flat, phased, grad_flat, grad_phased, totals):
    half_rows = grad_ref.shape[0] // 2
    spread(padded_ref, flat, phased, 4 * PHASES)
    spread(grad_ref, grad_flat, grad_phased, PHASES)
    totals[...] = jnp.zeros_like(totals)

    def block(index, carry):
        parity = lax.rem(index, 2)
        phase = lax.div(index, 2)
        grads = [grad_phased[parity + 2 * row, phase] for row in range(half_rows)]
        for tap_col in range(KSIZE):
            sums = [totals[KSIZE * a + tap_col] for a in range(KSIZE)]
            for row in range(half_rows + KSIZE - 1):
                window = phased[parity + 2 * row, phase + DILATE * tap_col]
                for a in range(KSIZE):
                    if 0 <= row - a < half_rows:
                        sums[a] = sums[a] + grads[row - a] * window
            for a in range(KSIZE):
                totals[KSIZE * a + tap_col] = sums[a]
        return carry

    lax.fori_loop(0, 2 * PHASES, block, 0)
    out_ref[...] = jnp.sum(totals[...], axis=1)


def stencil_cost(rows, cols, channels):
    return pl.CostEstimate(
        flops=2 * TAPS * rows * cols * channels,
        bytes_accessed=8 * rows * cols * channels,
        transcendentals=0,
    )


def stencil_call(kernel, padded, taps, extra, tile_shape):
    rows, cols, channels = tile_shape
    padded_rows, padded_cols, _ = padded.shape
    field = lambda h, w: pl.BlockSpec((h, w, LANES), lambda c: (0, 0, c))
    return pl.pallas_call(
        kernel,
        grid=(channels // LANES,),
        out_shape=jax.ShapeDtypeStruct(tile_shape, jnp.bfloat16),
        in_specs=[
            field(padded_rows, padded_cols),
            pl.BlockSpec((TAPS, LANES), lambda c: (0, c)),
        ]
        + [field(rows, cols)] * len(extra),
        out_specs=field(rows, cols),
        scratch_shapes=[
            pltpu.VMEM((padded_rows, padded_cols, LANES), jnp.float32),
            pltpu.VMEM((padded_rows, 4 * PHASES, 8, LANES), jnp.float32),
            pltpu.VMEM((rows, cols, LANES), jnp.float32),
        ],
        compiler_params=pltpu.CompilerParams(vmem_limit_bytes=VMEM_BYTES),
        cost_estimate=stencil_cost(rows, cols, channels),
    )(padded, taps, *extra)


def taps_call(padded, grad):
    rows, cols, channels = grad.shape
    padded_rows, padded_cols, _ = padded.shape
    field = lambda h, w: pl.BlockSpec((h, w, LANES), lambda c: (0, 0, c))
    return pl.pallas_call(
        taps_kernel,
        grid=(channels // LANES,),
        out_shape=jax.ShapeDtypeStruct((TAPS, channels), jnp.float32),
        in_specs=[field(padded_rows, padded_cols), field(rows, cols)],
        out_specs=pl.BlockSpec((TAPS, LANES), lambda c: (0, c)),
        scratch_shapes=[
            pltpu.VMEM((padded_rows, padded_cols, LANES), jnp.float32),
            pltpu.VMEM((padded_rows, 4 * PHASES, 8, LANES), jnp.float32),
            pltpu.VMEM((rows, cols, LANES), jnp.float32),
            pltpu.VMEM((rows, PHASES, 8, LANES), jnp.float32),
            pltpu.VMEM((TAPS, 8, LANES), jnp.float32),
        ],
        compiler_params=pltpu.CompilerParams(vmem_limit_bytes=VMEM_BYTES),
        cost_estimate=stencil_cost(rows, cols, channels),
    )(padded, grad)


def standardize(conv):
    values = conv.astype(jnp.float32)
    centered = values - jnp.mean(values, axis=1, keepdims=True)
    inverse = lax.rsqrt(jnp.mean(centered * centered, axis=1, keepdims=True) + EPSILON)
    return centered * inverse, inverse


ROW_TILE = 128


def mlp_kernel(
    conv_ref, image_ref, cot_ref, gain_ref, layer_ref, bias_ref, w_in_ref, w_out_ref,
    out_ref, grad_conv_ref, grad_in_ref, grad_out_ref, bias_sum_ref, gain_sum_ref, scale_sum_ref,
    normed, normed_t, grad_mix, mixed, grad_norm, hidden, grad_pre,
):
    step = pl.program_id(0)
    pixels = normed.shape[0]
    tiles = [pl.ds(start, ROW_TILE) for start in range(0, pixels, ROW_TILE)]

    @pl.when(step == 0)
    def _():
        for tile in tiles:
            standard, _ = standardize(conv_ref[tile, :])
            rounded = (standard * gain_ref[...]).astype(jnp.bfloat16)
            normed[tile, :] = rounded
            normed_t[:, tile] = rounded.T
            grad_mix[tile, :] = (cot_ref[tile, :].astype(jnp.float32) * layer_ref[...]).astype(
                jnp.bfloat16
            )
        mixed[...] = jnp.zeros_like(mixed)
        grad_norm[...] = jnp.zeros_like(grad_norm)

    bias_total = jnp.zeros(bias_sum_ref.shape, jnp.float32)
    for tile in tiles:
        preact = dot(normed[tile, :], w_in_ref[...]) + bias_ref[...]
        grad_hidden = dot(grad_mix[tile, :], w_out_ref[...], CONTRACT_COLS)
        cdf = 0.5 * (1.0 + lax.erf(preact * 0.7071067811865476))
        slope = cdf + preact * jnp.exp(-0.5 * preact * preact) * 0.3989422804014327
        grad_value = grad_hidden * slope
        bias_total = bias_total + jnp.sum(grad_value, axis=0, keepdims=True)
        hidden_tile = (preact * cdf).astype(jnp.bfloat16)
        pre_tile = grad_value.astype(jnp.bfloat16)
        hidden[tile, :] = hidden_tile
        grad_pre[tile, :] = pre_tile
        mixed[tile, :] += dot(hidden_tile, w_out_ref[...])
        grad_norm[tile, :] += dot(pre_tile, w_in_ref[...], CONTRACT_COLS)
    bias_sum_ref[...] = bias_total
    grad_in_ref[...] = dot(normed_t[...], grad_pre[...]).astype(grad_in_ref.dtype)
    grad_out_ref[...] = dot(hidden[...], grad_mix[...], CONTRACT_ROWS).astype(grad_out_ref.dtype)

    @pl.when(step == pl.num_programs(0) - 1)
    def _():
        gain_total = jnp.zeros(gain_sum_ref.shape, jnp.float32)
        scale_total = jnp.zeros(scale_sum_ref.shape, jnp.float32)
        for tile in tiles:
            mix = mixed[tile, :]
            out_ref[tile, :] = (
                image_ref[tile, :].astype(jnp.float32) + layer_ref[...] * mix
            ).astype(jnp.bfloat16)
            scale_total = scale_total + jnp.sum(
                cot_ref[tile, :].astype(jnp.float32) * mix, axis=0, keepdims=True
            )
            standard, inverse = standardize(conv_ref[tile, :])
            grad = grad_norm[tile, :]
            gain_total = gain_total + jnp.sum(grad * standard, axis=0, keepdims=True)
            scaled = grad * gain_ref[...]
            grad_conv_ref[tile, :] = (
                (
                    scaled
                    - jnp.mean(scaled, axis=1, keepdims=True)
                    - standard * jnp.mean(scaled * standard, axis=1, keepdims=True)
                )
                * inverse
            ).astype(jnp.bfloat16)
        gain_sum_ref[...] = gain_total
        scale_sum_ref[...] = scale_total


def mlp_call(conv, image, cot, gain, layer, bias, w_in, w_out, grad_type, chunk=256):
    pixels, channels = conv.shape
    hidden_units = w_out.shape[0]
    quarter_steps = hidden_units // (4 * chunk)
    quartered = pl.BlockSpec(
        (None, channels, chunk), lambda s: (s // quarter_steps, 0, s % quarter_steps)
    )
    whole = lambda h, w: pl.BlockSpec((h, w), lambda s: (0, 0))
    f32 = lambda *shape: jax.ShapeDtypeStruct(shape, jnp.float32)
    bf16 = lambda *shape: jax.ShapeDtypeStruct(shape, jnp.bfloat16)
    return pl.pallas_call(
        mlp_kernel,
        grid=(hidden_units // chunk,),
        out_shape=(
            bf16(pixels, channels),
            bf16(pixels, channels),
            jax.ShapeDtypeStruct((4, channels, hidden_units // 4), grad_type),
            jax.ShapeDtypeStruct((hidden_units, channels), grad_type),
            f32(1, hidden_units),
            f32(1, channels),
            f32(1, channels),
        ),
        in_specs=[
            whole(pixels, channels),
            whole(pixels, channels),
            whole(pixels, channels),
            whole(1, channels),
            whole(1, channels),
            pl.BlockSpec((1, chunk), lambda s: (0, s)),
            quartered,
            pl.BlockSpec((chunk, channels), lambda s: (s, 0)),
        ],
        out_specs=(
            whole(pixels, channels),
            whole(pixels, channels),
            quartered,
            pl.BlockSpec((chunk, channels), lambda s: (s, 0)),
            pl.BlockSpec((1, chunk), lambda s: (0, s)),
            whole(1, channels),
            whole(1, channels),
        ),
        scratch_shapes=[
            pltpu.VMEM((pixels, channels), jnp.bfloat16),
            pltpu.VMEM((channels, pixels), jnp.bfloat16),
            pltpu.VMEM((pixels, channels), jnp.bfloat16),
            pltpu.VMEM((pixels, channels), jnp.float32),
            pltpu.VMEM((pixels, channels), jnp.float32),
            pltpu.VMEM((pixels, chunk), jnp.bfloat16),
            pltpu.VMEM((pixels, chunk), jnp.bfloat16),
        ],
        compiler_params=pltpu.CompilerParams(vmem_limit_bytes=VMEM_BYTES),
        cost_estimate=pl.CostEstimate(
            flops=12 * pixels * channels * hidden_units,
            bytes_accessed=12 * channels * hidden_units,
            transcendentals=2 * pixels * hidden_units,
        ),
    )(conv, image, cot, gain, layer, bias, w_in, w_out)


MESH = pl.DeviceIdType.MESH
PARTS = 2


class Place:
    def __init__(self):
        self.row = lax.axis_index("row")
        self.col = lax.axis_index("col")
        self.depth = lax.axis_size("col") // 4
        self.z = self.col // 4
        self.y = (self.col // 2) % 2
        self.x = self.col % 2
        self.core = self.row % 2

    def at(self, z, y, x):
        return (self.row, 4 * z + 2 * y + x)

    def z_peer(self, hop):
        return self.at((self.z + hop) % self.depth, self.y, self.x)

    def y_peer(self):
        return self.at(self.z, 1 - self.y, self.x)

    def x_peer(self):
        return self.at(self.z, self.y, 1 - self.x)

    def core_peer(self):
        return (self.row + 1 - 2 * self.core, self.col)

    def greet(self):
        barrier = pltpu.get_barrier_semaphore()
        peers = [self.z_peer(hop) for hop in range(1, self.depth)]
        peers += [self.y_peer(), self.x_peer(), self.core_peer()]
        for peer in peers:
            pl.semaphore_signal(barrier, inc=1, device_id=peer, device_id_type=MESH)
        pl.semaphore_wait(barrier, len(peers))


class Mail:
    def __init__(self, send_sems, recv_sems):
        self.send_sems, self.recv_sems, self.copies = send_sems, recv_sems, []

    def send(self, source, target, peer):
        slot = len(self.copies)
        copy = pltpu.make_async_remote_copy(
            src_ref=source,
            dst_ref=target,
            send_sem=self.send_sems.at[slot],
            recv_sem=self.recv_sems.at[slot],
            device_id=peer,
            device_id_type=MESH,
        )
        copy.start()
        self.copies.append(copy)
        return copy

    def finish(self):
        for copy in self.copies:
            copy.wait_send()


def gather_kernel(
    shard_in, shard_out, padded_ref, taps_ref, full_in, full_out, conv_ref,
    send_sems, recv_sems, own_sems, flat, phased, summed,
):
    place = Place()
    z, y, x = place.z, place.y, place.x
    mine = pl.ds(2 * place.core, 2)
    own_in = pltpu.make_async_copy(shard_in.at[mine], full_in.at[mine, z, y, x], own_sems.at[0])
    own_out = pltpu.make_async_copy(
        shard_out.at[mine], full_out.at[z, y, x, mine], own_sems.at[1]
    )
    own_in.start()
    own_out.start()
    place.greet()
    own_in.wait()
    own_out.wait()
    mail = Mail(send_sems, recv_sems)
    every = slice(None)

    def view(array, quarter, zs, ys, xs):
        if array == 0:
            return full_in.at[quarter, zs, ys, xs]
        return full_out.at[zs, ys, xs, quarter]

    def send(piece, stage):
        array, part = piece
        quarter = 2 * place.core + part
        first_y = part == 0
        if stage == 0:
            block = view(array, quarter, z, y, x)
            return [mail.send(block, block, place.z_peer(hop)) for hop in range(1, place.depth)]
        if stage == 1:
            block = view(array, quarter, every, y, x)
            return [mail.send(block, block, place.y_peer() if first_y else place.x_peer())]
        if stage == 2:
            block = view(array, quarter, every, *((every, x) if first_y else (y, every)))
            return [mail.send(block, block, place.x_peer() if first_y else place.y_peer())]
        block = view(array, quarter, every, every, every)
        return [mail.send(block, block, place.core_peer())]

    pieces = [(array, part) for array in range(2) for part in range(PARTS)]
    flying = [[] for _ in pieces]
    blocks = list(range(0, conv_ref.shape[2], LANES))
    for tick in range(len(pieces) // PARTS + 4):
        for index in range(len(pieces)):
            stage = tick - index // PARTS
            if 0 <= stage <= 4:
                for copy in flying[index]:
                    copy.wait_recv()
                if stage < 4:
                    flying[index] = send(pieces[index], stage)
        for start in blocks[2 * tick : 2 * tick + 2]:
            lanes = pl.ds(start, LANES)
            forward_block(
                padded_ref.at[:, :, lanes], taps_ref.at[:, lanes], conv_ref.at[:, :, lanes],
                flat, phased, summed,
            )
    mail.finish()


def gather_call(w_in, w_out, padded, taps, tile_shape):
    depth = lax.axis_size("col") // 4
    in_rows, hidden_units = w_in.shape
    out_rows, channels = w_out.shape
    width, height = hidden_units // 4, out_rows // 4
    shard_in = w_in.reshape(in_rows, 4, width).transpose(1, 0, 2)
    shard_out = w_out.reshape(4, height, channels)
    copies = 4 * (depth - 1 + 3)
    anywhere = pl.BlockSpec(memory_space=pl.ANY)
    vmem = pl.BlockSpec(memory_space=pltpu.VMEM)
    padded_rows, padded_cols, _ = padded.shape
    full_in, full_out, conv = pl.pallas_call(
        gather_kernel,
        out_shape=(
            jax.ShapeDtypeStruct((4, depth, 2, 2, in_rows, width), w_in.dtype),
            jax.ShapeDtypeStruct((depth, 2, 2, 4, height, channels), w_out.dtype),
            jax.ShapeDtypeStruct(tile_shape, jnp.bfloat16),
        ),
        in_specs=[anywhere, anywhere, vmem, vmem],
        out_specs=(anywhere, anywhere, vmem),
        scratch_shapes=[
            pltpu.SemaphoreType.DMA((copies,)),
            pltpu.SemaphoreType.DMA((copies,)),
            pltpu.SemaphoreType.DMA((2,)),
            pltpu.VMEM((padded_rows, padded_cols, LANES), jnp.float32),
            pltpu.VMEM((padded_rows, 4 * PHASES, 8, LANES), jnp.float32),
            pltpu.VMEM(tile_shape[:2] + (LANES,), jnp.float32),
        ],
        compiler_params=pltpu.CompilerParams(
            collective_id=0, has_side_effects=True, vmem_limit_bytes=VMEM_BYTES
        ),
    )(shard_in, shard_out, padded, taps)
    full_in = full_in.reshape(4, 4 * depth * in_rows, width)
    return full_in, full_out.reshape(-1, channels), conv


def scatter_kernel(
    grad_in, grad_out, small, total, small_total,
    recv_core, sum_core, recv_one, sum_one, recv_two, sum_two, recv_z, small_pair, small_z,
    send_sems, recv_sems,
):
    place = Place()
    z, y, x = place.z, place.y, place.x
    depth = place.depth
    place.greet()
    mail = Mail(send_sems, recv_sems)
    f32 = jnp.float32
    every = slice(None)

    def block_of(array, quarter, zz, yy, xx):
        if array == 0:
            return grad_in.at[quarter, zz, yy, xx]
        return grad_out.at[zz, yy, xx, quarter]

    pieces = [(array, part) for array in range(2) for part in range(PARTS)]
    small_copy = mail.send(small, small_pair.at[0], place.core_peer())
    flying = []
    for index, (array, part) in enumerate(pieces):
        source = block_of(array, 2 * (1 - place.core) + part, every, every, every)
        flying.append([mail.send(source, recv_core.at[index], place.core_peer())])

    def add(target, left, right):
        target[...] = (left[...].astype(f32) + right[...].astype(f32)).astype(target.dtype)

    def advance(index, stage):
        array, part = pieces[index]
        quarter = 2 * place.core + part
        x_first = part == 0
        near, far = (x, y) if x_first else (y, x)
        near_peer, far_peer = place.x_peer(), place.y_peer()
        if not x_first:
            near_peer, far_peer = far_peer, near_peer
        for copy in flying[index]:
            copy.wait_recv()
        if stage == 0:

            def add_core(zz, carry):
                for yy in range(2):
                    for xx in range(2):
                        first, second = (xx, yy) if x_first else (yy, xx)
                        add(
                            sum_core.at[index, first, zz, second],
                            block_of(array, quarter, zz, yy, xx),
                            recv_core.at[index, zz, yy, xx],
                        )
                return carry

            lax.fori_loop(0, depth, add_core, 0)
            return [mail.send(sum_core.at[index, 1 - near], recv_one.at[index], near_peer)]
        if stage == 1:

            def add_one(zz, carry):
                for second in range(2):
                    add(
                        sum_one.at[index, second, zz],
                        sum_core.at[index, near, zz, second],
                        recv_one.at[index, zz, second],
                    )
                return carry

            lax.fori_loop(0, depth, add_one, 0)
            return [mail.send(sum_one.at[index, 1 - far], recv_two.at[index], far_peer)]
        if stage == 2:

            def add_two(zz, carry):
                add(
                    sum_two.at[index, zz],
                    sum_one.at[index, far, zz],
                    recv_two.at[index, zz],
                )
                return carry

            lax.fori_loop(0, depth, add_two, 0)
            return [
                mail.send(
                    sum_two.at[index, (z + hop) % depth],
                    recv_z.at[index, hop - 1],
                    place.z_peer(hop),
                )
                for hop in range(1, depth)
            ]
        if stage == 3:
            owned = sum_two[index, z].astype(f32)
            for hop in range(1, depth):
                owned = owned + recv_z[index, hop - 1].astype(f32)
            total[array, quarter] = owned
            block = total.at[array, quarter]
            return [mail.send(block, block, place.core_peer())]
        return []

    def advance_small(stage):
        if stage < 3:
            small_flying[0].wait_recv()
            source = small if stage == 0 else small_pair.at[2 + stage]
            if stage < 2:
                add(small_pair.at[3 + stage], source, small_pair.at[stage])
                peer = place.x_peer() if stage == 0 else place.y_peer()
                return [mail.send(small_pair.at[3 + stage], small_pair.at[1 + stage], peer)]
            add(small_z.at[0], source, small_pair.at[stage])
            return [
                mail.send(small_z.at[0], small_z.at[hop], place.z_peer(hop))
                for hop in range(1, depth)
            ]
        for copy in small_flying:
            copy.wait_recv()
        summed = small_z[z]
        for other in range(1, depth):
            summed = summed + small_z[(z + depth - other) % depth]
        small_total[...] = summed
        return []

    small_flying = [small_copy]
    for tick in range(len(pieces) // PARTS + 4):
        for index in range(len(pieces)):
            if 0 <= tick - index // PARTS <= 4:
                flying[index] = advance(index, tick - index // PARTS)
        if tick < 4:
            small_flying = advance_small(tick)
    mail.finish()


def scatter_call(grad_in, grad_out, small):
    depth = lax.axis_size("col") // 4
    _, channels, width = grad_in.shape
    height = channels // (4 * depth)
    grad_in = grad_in.reshape(4, depth, 2, 2, height, width)
    grad_out = grad_out.reshape(depth, 2, 2, 4, -1, channels)
    assert grad_out.shape[4:] == (height, width)
    kind = grad_in.dtype
    vmem = pl.BlockSpec(memory_space=pltpu.VMEM)
    copies = 4 * (1 + 1 + 1 + depth - 1 + 1) + 3 + depth - 1
    return pl.pallas_call(
        scatter_kernel,
        out_shape=(
            jax.ShapeDtypeStruct((2, 4, height, width), jnp.float32),
            jax.ShapeDtypeStruct(small.shape, jnp.float32),
        ),
        in_specs=[vmem] * 3,
        out_specs=(vmem, vmem),
        scratch_shapes=[
            pltpu.VMEM((4, depth, 2, 2, height, width), kind),
            pltpu.VMEM((4, 2, depth, 2, height, width), kind),
            pltpu.VMEM((4, depth, 2, height, width), kind),
            pltpu.VMEM((4, 2, depth, height, width), kind),
            pltpu.VMEM((4, depth, height, width), kind),
            pltpu.VMEM((4, depth, height, width), kind),
            pltpu.VMEM((4, depth - 1, height, width), kind),
            pltpu.VMEM((5,) + small.shape, jnp.float32),
            pltpu.VMEM((depth,) + small.shape, jnp.float32),
            pltpu.SemaphoreType.DMA((copies,)),
            pltpu.SemaphoreType.DMA((copies,)),
        ],
        compiler_params=pltpu.CompilerParams(
            collective_id=1, has_side_effects=True, vmem_limit_bytes=VMEM_BYTES
        ),
    )(grad_in, grad_out, small)


def local(image, dw_kernel, ln_gain, w_in, b_in, w_out, layer_scale, cotangent):
    tile_shape = image.shape
    tile_rows, tile_cols, channels = tile_shape
    group_count = lax.axis_size("row") * lax.axis_size("col")
    pixels = tile_rows * tile_cols
    scale_factor = 1.0 / math.sqrt(pixels * group_count)
    flat = lambda field: field.reshape(pixels, channels)
    taps = dw_kernel.T
    padded = halo_pad(image)
    full_in, full_out, conv = gather_call(w_in, w_out, padded, taps, tile_shape)
    out_map, grad_conv, grad_in, grad_out, bias_part, gain_part, scale_part = mlp_call(
        flat(conv),
        flat(image),
        flat(cotangent),
        ln_gain[None],
        layer_scale[None],
        b_in[None],
        full_in,
        full_out,
        jnp.bfloat16,
    )
    grad_conv = grad_conv.reshape(tile_shape)
    grad_padded = halo_pad(grad_conv)
    tap_part = taps_call(padded, grad_conv)
    grad_image = stencil_call(backward_kernel, grad_padded, taps[::-1], (cotangent,), tile_shape)
    small_rows = [tap_part, bias_part.reshape(-1, channels), gain_part, scale_part]
    small = jnp.concatenate(small_rows, axis=0)
    small = jnp.pad(small, ((0, -small.shape[0] % 8), (0, 0)))
    total, small_total = scatter_call(grad_in, grad_out, small)
    if lax.axis_size("row") > 2:
        total, small_total = (0.5 * field for field in lax.psum((total, small_total), "row"))
    summed_in = total[0].transpose(1, 0, 2).reshape(w_in.shape)
    summed_out = total[1].reshape(w_out.shape)
    tap_sum = small_total[:TAPS]
    rows_used = TAPS + bias_part.size // channels
    bias_sum = small_total[TAPS:rows_used].reshape(-1)
    gain_sum, scale_sum = small_total[rows_used], small_total[rows_used + 1]
    group_size = channels // group_count
    group_index = lax.axis_index("row") * lax.axis_size("col") + lax.axis_index("col")
    grad_kernel = lax.dynamic_slice_in_dim(tap_sum.T, group_index * group_size, group_size, 0)
    return (
        out_map.reshape(tile_shape),
        grad_image,
        grad_kernel * scale_factor,
        summed_in * scale_factor,
        summed_out * scale_factor,
        bias_sum * scale_factor,
        gain_sum * scale_factor,
        scale_sum * scale_factor,
    )


def solution(mesh):
    in_specs = (
        P("row", "col", None),
        P(),
        P(),
        P("col", None),
        P(),
        P("col", None),
        P(),
        P("row", "col", None),
    )
    out_specs = (
        P("row", "col", None),
        P("row", "col", None),
        P(("row", "col"), None),
        P("col", None),
        P("col", None),
        P(),
        P(),
        P(),
    )
    return jax.shard_map(local, mesh=mesh, in_specs=in_specs, out_specs=out_specs, check_vma=False)
```
